32 devices in a mesh: dp: 8 (over z, x), tensor: 4 (over y, core).
Axes of the slice: x: 2, y: 2, z: 4, core: 2. Of those that a mesh axis runs over, the one named last changes fastest.
Arguments:
- tokens: bfloat16 [32768, 1024], P('dp'), may hold values from -6 to 6
- lengths: int32 [64], P('dp'), may hold values from 1 to 512, 24576 in all
- qkv_weight: bfloat16 [3, 1024, 1024], P(None, 'dp', 'tensor'), may hold values from -0.1875 to 0.1875
- qv_bias: bfloat16 [2, 16, 64], P(None, 'tensor', 'dp'), may hold values from -2 to 2
- out_weight: bfloat16 [1024, 1024], P('tensor', 'dp'), may hold values from -2 to 2
- out_bias: bfloat16 [1024], P('dp'), may hold values from -2 to 2
- up_weight: bfloat16 [1024, 4096], P('dp', 'tensor'), may hold values from -0.1875 to 0.1875
- up_bias: bfloat16 [64, 64], P('tensor', 'dp'), may hold values from -3 to 3
- down_weight: bfloat16 [4096, 1024], P('tensor', 'dp'), may hold values from -0.09375 to 0.09375
- down_bias: bfloat16 [1024], P('dp'), may hold values from -2 to 2
- norm_gain: bfloat16 [2, 1024], P(None, 'dp'), may hold values from 0.5 to 1.5
- norm_shift: bfloat16 [2, 1024], P(None, 'dp'), may hold values from -2 to 2
- cotangent: bfloat16 [32768, 1024], P('dp'), may hold values from -6 to 6
Outputs:
- out: bfloat16 [32768, 1024], P(('dp', 'tensor'))
- in_grad: float32 [32768, 1024], P(('dp', 'tensor'))
- qkv_weight_grad: float32 [3, 1024, 1024], P(None, 'dp', 'tensor')
- qv_bias_grad: float32 [2, 16, 64], P(None, 'tensor', 'dp')
- out_weight_grad: float32 [1024, 1024], P('tensor', 'dp')
- out_bias_grad: float32 [1024], P('dp')
- up_weight_grad: float32 [1024, 4096], P('dp', 'tensor')
- up_bias_grad: float32 [64, 64], P('tensor', 'dp')
- down_weight_grad: float32 [4096, 1024], P('tensor', 'dp')
- down_bias_grad: float32 [1024], P('dp')
- norm_gain_grad: float32 [2, 1024], P(None, 'dp')
- norm_shift_grad: float32 [2, 1024], P(None, 'dp')
The draws below stay inside these ranges and needn't reach their ends.
All inputs are finite; a program needn't handle non-finite values. No bound on the sum of `lengths` on one device may be relied on, other than what follows from the above.
Results may differ from the reference program's by a relative error of at most 0.02.
Values may be sent and summed in bfloat16 or wider, within the bound.
A program may use at most 320 MiB of HBM per device.

```python
import math
import jax
import jax.numpy as jnp
import numpy as np
from jax import lax

D = 1024
HEADS = 16
HD = 64
FF = 4096
SEQ = 512
SLOTS = 8
SEQS = 64
TOKENS = 32768
N_DP = 8
N_TENSOR = 4


def level_of(own_key, dims, cuts, low, largest):
    def one(dim, parts):
        steps = jax.random.uniform(jax.random.fold_in(jax.random.fold_in(own_key, 6), dim), (parts,), jnp.float32, low / len(cuts), largest / len(cuts))
        return jnp.repeat(jnp.exp(steps), dims[dim] // parts).reshape((-1,) + (1,) * (len(dims) - dim - 1))

    gain = one(*cuts[0])
    for cut in cuts[1:]:
        gain = gain * one(*cut)
    return gain


def split_up(number_of, total, bound, slope):
    loads = [(1 << 20) // math.isqrt(standing ** slope) + 1 for standing in range(2, number_of + 1)]
    rest, holding = total - bound - (number_of - 1), [1] * (number_of - 1)
    while rest > 0:
        free = [i for i in range(number_of - 1) if holding[i] < bound]
        mass, remaining = sum([loads[i] for i in free]), rest
        for i in free:
            addition = min(bound - holding[i], max(1, remaining * loads[i] // mass), rest)
            holding[i] = holding[i] + addition
            rest = rest - addition
    return np.array([bound] + holding)


def uneven(rng, amount, total, most, slope):
    if amount == 2:
        one = jax.random.randint(rng, (), max(1, total - most), min(most, total - 1) + 1)
        return jnp.stack([one, total - one])
    sizes = jnp.asarray(split_up(amount, total, most, slope), jnp.int32)
    couples = (amount - 1) // 2
    giver, sink = sizes[1:1 + 2 * couples:2], sizes[2:2 + 2 * couples:2]
    margin = jnp.minimum(giver - 1, most - sink)
    passed = jax.random.randint(jax.random.fold_in(rng, 1), (couples,), 0, 1 << 20) % (margin + 1)
    sizes = sizes.at[1:1 + 2 * couples:2].set(giver - passed).at[2:2 + 2 * couples:2].set(sink + passed)
    return sizes[jax.random.permutation(jax.random.fold_in(rng, 2), amount)]


def gaussian(own_key, dims, scale, reach, split=(), kind=jnp.bfloat16):
    drawn = scale * jax.random.normal(own_key, dims, jnp.float32)
    if split:
        drawn = drawn * level_of(own_key, dims, split, -0.22, 0.18)
    return jnp.clip(drawn, -reach, reach).astype(kind)


def setup_inputs(seed: int = 0) -> dict:
    key_of = jax.random.split(jax.random.key(seed), 14)
    tokens = gaussian(key_of[0], (TOKENS, D), 1.0, 6.0, ((0, 8),))
    lengths = uneven(key_of[1], SEQS, SEQS * SEQ * 3 // 4, SEQ, 1).astype(jnp.int32)
    qkv_weight = gaussian(key_of[2], (3, D, D), D ** -0.5, 0.1875, ((1, 8), (2, 4)))
    qv_bias = gaussian(key_of[3], (2, HEADS, HD), 0.3, 2.0, ((1, 4), (2, 8)))
    out_weight = gaussian(key_of[4], (D, D), (D * 4 // SEQ) ** -0.5, 2.0, ((0, 4), (1, 8)))
    out_bias = gaussian(key_of[5], (D,), 0.3, 2.0, ((0, 8),))
    up_weight = gaussian(key_of[6], (D, FF), D ** -0.5, 0.1875, ((0, 8), (1, 4)))
    up_bias = gaussian(key_of[7], (FF // HD, HD), 0.5, 3.0, ((0, 4), (1, 8)))
    down_weight = gaussian(key_of[8], (FF, D), FF ** -0.5, 0.09375, ((0, 4), (1, 8)))
    down_bias = gaussian(key_of[9], (D,), 0.3, 2.0, ((0, 8),))
    norm_gain = jnp.clip(1.0 + 0.1 * jax.random.normal(key_of[10], (2, D), jnp.float32), 0.5, 1.5).astype(jnp.bfloat16)
    norm_shift = gaussian(key_of[11], (2, D), 0.3, 2.0, ((1, 8),))
    cotangent = gaussian(key_of[12], (TOKENS, D), 1.0, 6.0, ((0, 8),))
    return {"tokens": tokens, "lengths": lengths, "qkv_weight": qkv_weight, "qv_bias": qv_bias, "out_weight": out_weight, "out_bias": out_bias, "up_weight": up_weight, "up_bias": up_bias, "down_weight": down_weight, "down_bias": down_bias, "norm_gain": norm_gain, "norm_shift": norm_shift, "cotangent": cotangent}


@jax.custom_vjp
def low(v):
    return lax.optimization_barrier(v.astype(jnp.bfloat16)).astype(jnp.float32)

@jax.custom_vjp
def low_back(v):
    return v

def low_keep(v):
    return (low(v), None)

def low_pass(kept, grad):
    return (grad,)

def back_keep(v):
    return (v, None)

def back_low(kept, grad):
    return (low(grad),)
low.defvjp(low_keep, low_pass)
low_back.defvjp(back_keep, back_low)
HIGHEST = lax.Precision.HIGHEST

def round_both(operand):
    return low(low_back(operand))

def normalize(summed, gain_row, shift_row):
    row_mean = lax.optimization_barrier(jnp.mean(summed, axis=-1, keepdims=True))
    centred = summed - row_mean
    return centred * lax.rsqrt(lax.optimization_barrier(jnp.mean(centred * centred, axis=-1, keepdims=True)) + 1e-05) * gain_row + shift_row

def encoder_layer(weight_set, token_rows, key_valid):
    qkv_weight, qv_bias, out_weight, out_bias, up_weight, up_bias, down_weight, down_bias, norm_gain, norm_shift = weight_set
    row_count = token_rows.shape[0]
    seq_count = row_count // SEQ
    head_width = D // N_TENSOR
    ffn_width = FF // N_TENSOR
    spread_in = low_back(jnp.broadcast_to(token_rows[:, None, :], (row_count, N_TENSOR, D)))
    projected = jnp.einsum('rtd,cdtk->crtk', spread_in, qkv_weight.reshape(3, D, N_TENSOR, head_width), precision=HIGHEST)
    projected = projected.reshape(3, row_count, D)
    qv_flat = qv_bias.reshape(2, D)
    queries = round_both(projected[0] + qv_flat[0]).reshape(seq_count, SEQ, HEADS, HD)
    key_heads = round_both(projected[1]).reshape(seq_count, SEQ, HEADS, HD)
    values = round_both(projected[2] + qv_flat[1]).reshape(seq_count, SEQ, HEADS, HD)
    scores = jnp.einsum('sihe,sjhe->shij', queries, key_heads, precision=HIGHEST) * HD ** (-0.5)
    scores = low_back(jnp.where(key_valid[:, None, None, :] > 0, scores, -1000000000.0))
    attention = low(jax.nn.softmax(scores, axis=-1))
    context = jnp.einsum('shij,sjhe->sihe', attention, values, precision=HIGHEST)
    context = round_both(context.reshape(row_count, D))
    partials = jnp.einsum('rtk,tkd->rtd', context.reshape(row_count, N_TENSOR, head_width), out_weight.reshape(N_TENSOR, head_width, D), precision=HIGHEST)
    attended = low_back(lax.optimization_barrier(jnp.sum(low(partials), axis=1)))
    normed_one = normalize(token_rows + attended + out_bias, norm_gain[0], norm_shift[0])
    spread_mid = low_back(jnp.broadcast_to(low(normed_one)[:, None, :], (row_count, N_TENSOR, D)))
    pre_act = jnp.einsum('rtd,dtf->rtf', spread_mid, up_weight.reshape(D, N_TENSOR, ffn_width), precision=HIGHEST)
    pre_act = low_back(pre_act + up_bias.reshape(N_TENSOR, ffn_width))
    hidden = low(jax.nn.gelu(pre_act, approximate=False))
    partials = jnp.einsum('rtf,tfd->rtd', hidden, down_weight.reshape(N_TENSOR, ffn_width, D), precision=HIGHEST)
    ffn_out = low_back(lax.optimization_barrier(jnp.sum(low(partials), axis=1)))
    return normalize(normed_one + ffn_out + down_bias, norm_gain[1], norm_shift[1])

def reference(tokens, lengths, qkv_weight, qv_bias, out_weight, out_bias, up_weight, up_bias, down_weight, down_bias, norm_gain, norm_shift, cotangent):
    weights_all = tuple((member.astype(jnp.float32) for member in (qkv_weight, qv_bias, out_weight, out_bias, up_weight, up_bias, down_weight, down_bias, norm_gain, norm_shift)))
    block_rows = SLOTS * SEQ
    positions = jnp.arange(SEQ, dtype=jnp.int32)
    pieces = (tokens.reshape(N_DP, block_rows, D), lengths.reshape(N_DP, SLOTS), cotangent.reshape(N_DP, block_rows, D))

    def block_step(totals, portion):
        token_rows, portion_lengths, portion_cot = portion
        key_valid = (positions[None, :] < portion_lengths[:, None]).astype(jnp.int32)

        def forward(weight_set, inputs):
            return encoder_layer(weight_set, inputs, key_valid)
        result, pullback = jax.vjp(forward, weights_all, token_rows.astype(jnp.float32))
        row_valid = key_valid.reshape(block_rows).astype(jnp.float32)
        weight_grads, input_grad = pullback(portion_cot.astype(jnp.float32) * row_valid[:, None])
        totals = jax.tree.map(lambda left, right: left + right, totals, weight_grads)
        return (totals, (result.astype(jnp.bfloat16), input_grad))
    empty_grads = jax.tree.map(jnp.zeros_like, weights_all)
    totals, (outputs, input_grads) = lax.scan(block_step, empty_grads, pieces)
    return (outputs.reshape(TOKENS, D), input_grads.reshape(TOKENS, D), totals[0], totals[1], totals[2], totals[3], totals[4], totals[5], totals[6], totals[7], totals[8], totals[9])
```

```python
import functools

import jax
import jax.numpy as jnp
from jax import lax
from jax.experimental import pallas as pl
from jax.experimental.pallas import tpu as pltpu
from jax.sharding import PartitionSpec as P

HD = 64
SEQ = 512
EPSILON = 1e-05
SCALE = HD ** (-0.5)
ALL = ("tensor", "dp")
F32 = jnp.float32
BF16 = jnp.bfloat16


def dot(left, right, left_dim, right_dim):
    return lax.dot_general(
        left, right, (((left_dim,), (right_dim,)), ((), ())), preferred_element_type=F32
    )


def head_part(ref, start):
    return ref[0, :, start : start + HD]


def attend_kernel(width, lengths_ref, proj_ref, context_ref, log_ref):
    length = lengths_ref[pl.program_id(1)]
    valid = lax.broadcasted_iota(jnp.int32, (SEQ, SEQ), 0) < length
    done = []
    for head in range(width // HD):
        at = head * HD
        query = head_part(proj_ref, at) * SCALE
        key = head_part(proj_ref, width + at)
        value = head_part(proj_ref, 2 * width + at)
        scores = jnp.where(valid, dot(key, query, 1, 1), -1000000000.0)
        top = jnp.max(scores, axis=0, keepdims=True)
        expo = jnp.exp(scores - top)
        total = jnp.sum(expo, axis=0, keepdims=True)
        probs = (expo * (1.0 / total)).astype(BF16)
        log_ref[0, 0, head : head + 1, :] = top + jnp.log(total)
        done.append(dot(value, probs, 0, 0))
        if len(done) == 2:
            pair = jnp.concatenate(done, axis=0)
            context_ref[0, :, at - HD : at + HD] = pair.T.astype(BF16)
            done = []


def attend_back_kernel(width, lengths_ref, proj_ref, log_ref, d_context_ref, out_ref):
    length = lengths_ref[pl.program_id(1)]
    valid = lax.broadcasted_iota(jnp.int32, (SEQ, SEQ), 0) < length
    d_query, d_key, d_value = [], [], []
    for head in range(width // HD):
        at = head * HD
        query = head_part(proj_ref, at) * SCALE
        key = head_part(proj_ref, width + at)
        value = head_part(proj_ref, 2 * width + at)
        d_context = head_part(d_context_ref, at)
        scores = jnp.where(valid, dot(key, query, 1, 1), -1000000000.0)
        probs = jnp.exp(scores - log_ref[0, 0, head : head + 1, :])
        d_probs = dot(value, d_context, 1, 1)
        inner = jnp.sum(probs * d_probs, axis=0, keepdims=True)
        d_scores = (probs * (d_probs - inner)).astype(BF16)
        d_query.append(dot(key, d_scores, 0, 0) * SCALE)
        d_key.append(dot(d_scores, query, 1, 0).astype(BF16))
        d_value.append(dot(probs.astype(BF16), d_context, 1, 0).astype(BF16))
        if len(d_query) == 2:
            low, high = at - HD, at + HD
            out_ref[0, :, low:high] = jnp.concatenate(d_query, axis=0).T.astype(BF16)
            out_ref[0, :, width + low : width + high] = jnp.concatenate(d_key, axis=1)
            out_ref[0, :, 2 * width + low : 2 * width + high] = jnp.concatenate(d_value, axis=1)
            d_query, d_key, d_value = [], [], []


def attend(lengths, projected):
    groups, rows, joint = projected.shape
    width = joint // 3
    heads = width // HD
    seqs = rows // SEQ
    return pl.pallas_call(
        functools.partial(attend_kernel, width),
        grid=(groups, seqs),
        in_specs=[
            pl.BlockSpec(memory_space=pltpu.SMEM),
            pl.BlockSpec((1, SEQ, joint), lambda t, s: (t, s, 0)),
        ],
        out_specs=[
            pl.BlockSpec((1, SEQ, width), lambda t, s: (t, s, 0)),
            pl.BlockSpec((1, 1, heads, SEQ), lambda t, s: (t, s, 0, 0)),
        ],
        out_shape=[
            jax.ShapeDtypeStruct((groups, rows, width), BF16),
            jax.ShapeDtypeStruct((groups, seqs, heads, SEQ), F32),
        ],
        compiler_params=pltpu.CompilerParams(vmem_limit_bytes=40 * 1024 * 1024),
        cost_estimate=pl.CostEstimate(
            flops=groups * seqs * heads * 16 * SEQ * SEQ * HD,
            bytes_accessed=groups * rows * joint * 3,
            transcendentals=groups * seqs * heads * SEQ * SEQ,
        ),
    )(lengths, projected)


def attend_back(lengths, projected, log_total, d_context):
    groups, rows, joint = projected.shape
    width = joint // 3
    heads = width // HD
    seqs = rows // SEQ
    return pl.pallas_call(
        functools.partial(attend_back_kernel, width),
        grid=(groups, seqs),
        in_specs=[
            pl.BlockSpec(memory_space=pltpu.SMEM),
            pl.BlockSpec((1, SEQ, joint), lambda t, s: (t, s, 0)),
            pl.BlockSpec((1, 1, heads, SEQ), lambda t, s: (t, s, 0, 0)),
            pl.BlockSpec((1, SEQ, width), lambda t, s: (t, s, 0)),
        ],
        out_specs=pl.BlockSpec((1, SEQ, joint), lambda t, s: (t, s, 0)),
        out_shape=jax.ShapeDtypeStruct((groups, rows, joint), BF16),
        compiler_params=pltpu.CompilerParams(vmem_limit_bytes=40 * 1024 * 1024),
        cost_estimate=pl.CostEstimate(
            flops=groups * seqs * heads * 40 * SEQ * SEQ * HD,
            bytes_accessed=groups * rows * joint * 5,
            transcendentals=groups * seqs * heads * SEQ * SEQ,
        ),
    )(lengths, projected, log_total, d_context)


def row_stats(summed):
    row_mean = jnp.mean(summed, axis=-1, keepdims=True)
    centred = summed - row_mean
    inverse = lax.rsqrt(jnp.mean(centred * centred, axis=-1, keepdims=True) + EPSILON)
    return centred * inverse, inverse


def norm_back(grad_rows, unit_rows, inverse, gain_row):
    scaled = grad_rows * gain_row
    inner = (
        scaled
        - jnp.mean(scaled, axis=-1, keepdims=True)
        - unit_rows * jnp.mean(scaled * unit_rows, axis=-1, keepdims=True)
    )
    return (
        inverse * inner,
        jnp.sum(grad_rows * unit_rows, axis=0),
        jnp.sum(grad_rows, axis=0),
    )


def spread(rows, matrices):
    return jnp.einsum("rd,tdn->trn", rows, matrices, preferred_element_type=F32)


def gather_in(parts, matrices):
    return jnp.einsum("trn,tdn->rd", parts, matrices, preferred_element_type=F32)


def outer(rows, parts):
    return jnp.einsum("rd,trn->tdn", rows, parts, preferred_element_type=F32).astype(BF16)


def per_device(
    tokens_all,
    lengths_all,
    qkv_weight,
    qv_bias,
    out_weight,
    out_bias,
    up_weight,
    up_bias,
    down_weight,
    down_bias,
    norm_gain,
    norm_shift,
    cotangent_all,
):
    groups, shares = lax.axis_size("tensor"), lax.axis_size("dp")
    depth, head_width = qkv_weight.shape[1:]
    width = depth * shares
    hidden_width = up_weight.shape[1]
    rows = tokens_all.shape[0] // groups
    seqs = rows // SEQ
    place = lax.axis_index("tensor")
    tokens = lax.dynamic_slice_in_dim(tokens_all, place * rows, rows, 0)
    cotangent = lax.dynamic_slice_in_dim(cotangent_all, place * rows, rows, 0)
    lengths = lax.dynamic_slice_in_dim(lengths_all, place * seqs, seqs, 0)

    def whole(block):
        full = lax.all_gather(block, ALL, axis=0, tiled=True)
        return full.reshape(groups, width, block.shape[1])

    qkv_block = jnp.transpose(qkv_weight, (1, 0, 2)).reshape(depth, 3 * head_width)
    qkv = whole(qkv_block)
    small_shapes = [
        qv_bias.shape, out_bias.shape, up_bias.shape,
        down_bias.shape, norm_gain.shape, norm_shift.shape,
    ]
    small = jnp.concatenate(
        [a.reshape(-1) for a in (qv_bias, out_bias, up_bias, down_bias, norm_gain, norm_shift)]
    )
    smalls = lax.all_gather(small, ALL, axis=0, tiled=False)
    smalls = smalls.reshape(groups, shares, small.shape[0]).astype(F32)
    cut, at = [], 0
    for shape in small_shapes:
        size = 1
        for length in shape:
            size *= length
        cut.append(smalls[:, :, at : at + size].reshape((groups, shares) + shape))
        at += size
    qv = jnp.transpose(cut[0], (0, 2, 3, 1, 4)).reshape(groups, 2, head_width)
    out_shift = cut[1][0].reshape(width)
    up_shift = jnp.transpose(cut[2], (0, 2, 1, 3)).reshape(groups, hidden_width)
    down_shift = cut[3][0].reshape(width)
    gains = jnp.transpose(cut[4][0], (1, 0, 2)).reshape(2, width)
    shifts = jnp.transpose(cut[5][0], (1, 0, 2)).reshape(2, width)

    rest = whole(jnp.concatenate([out_weight.T, up_weight, down_weight.T], axis=1))
    out_full = rest[:, :, :head_width]
    up_full = rest[:, :, head_width : head_width + hidden_width]
    down_full = rest[:, :, head_width + hidden_width :]

    qkv_bias = jnp.concatenate([qv[:, 0], jnp.zeros_like(qv[:, 0]), qv[:, 1]], axis=1)
    projected = (spread(tokens, qkv) + qkv_bias[:, None, :]).astype(BF16)
    context, log_total = attend(lengths, projected)

    attended = gather_in(context, out_full)
    unit_one, inverse_one = row_stats(tokens.astype(F32) + attended + out_shift)
    normed_one = unit_one * gains[0] + shifts[0]
    normed_one_b = normed_one.astype(BF16)
    pre_act = spread(normed_one_b, up_full) + up_shift[:, None, :]
    hidden = jax.nn.gelu(pre_act, approximate=False).astype(BF16)
    ffn_out = gather_in(hidden, down_full)
    unit_two, inverse_two = row_stats(normed_one + ffn_out + down_shift)
    out = (unit_two * gains[1] + shifts[1]).astype(BF16)

    positions = lax.iota(jnp.int32, SEQ)
    row_valid = (positions[None, :] < lengths[:, None]).astype(F32).reshape(rows, 1)
    d_out = cotangent.astype(F32) * row_valid
    d_sum_two, gain_two, shift_two = norm_back(d_out, unit_two, inverse_two, gains[1])
    d_ffn = d_sum_two.astype(BF16)
    down_bias_grad = jnp.sum(d_sum_two, axis=0)

    def owned(grad):
        flat = grad.reshape(groups * width, grad.shape[2])
        return lax.psum_scatter(flat, ALL, scatter_dimension=0, tiled=True).astype(F32)

    down_owned = owned(outer(d_ffn, hidden)).T
    d_hidden = spread(d_ffn, down_full)
    _, gelu_pull = jax.vjp(lambda inner: jax.nn.gelu(inner, approximate=False), pre_act)
    d_pre = gelu_pull(d_hidden)[0].astype(BF16)
    up_bias_grad = jnp.sum(d_pre.astype(F32), axis=1)
    up_grad = outer(normed_one_b, d_pre)
    d_normed_one = d_sum_two + gather_in(d_pre, up_full)
    d_sum_one, gain_one, shift_one = norm_back(d_normed_one, unit_one, inverse_one, gains[0])
    d_attn = d_sum_one.astype(BF16)
    out_bias_grad = jnp.sum(d_sum_one, axis=0)
    out_grad = outer(d_attn, context)
    d_context = spread(d_attn, out_full).astype(BF16)
    d_joined = attend_back(lengths, projected, log_total, d_context)
    qkv_grad = outer(tokens, d_joined)
    rest_owned = owned(jnp.concatenate([up_grad, out_grad, qkv_grad], axis=2))
    up_owned = rest_owned[:, :hidden_width]
    out_owned = rest_owned[:, hidden_width : hidden_width + head_width].T
    qkv_owned = jnp.transpose(
        rest_owned[:, hidden_width + head_width :].reshape(depth, 3, head_width), (1, 0, 2)
    )
    in_grad = d_sum_one + gather_in(d_joined, qkv)

    joined_sums = jnp.sum(d_joined.astype(F32), axis=1).reshape(groups, 3, head_width)
    qv_sums = jnp.stack([joined_sums[:, 0], joined_sums[:, 2]], axis=1)

    def per_owner(array, shape):
        return jnp.broadcast_to(array, (groups, shares) + shape).reshape(groups * shares, -1)

    heads, piece = qv_bias.shape[1:]
    unit_rows, unit_piece = up_bias.shape
    qv_sums = jnp.transpose(qv_sums.reshape(groups, 2, heads, shares, piece), (0, 3, 1, 2, 4))
    up_sums = jnp.transpose(up_bias_grad.reshape(groups, unit_rows, shares, unit_piece), (0, 2, 1, 3))
    two = lambda one, other: jnp.transpose(
        jnp.stack([one, other]).reshape(2, shares, depth), (1, 0, 2)
    )
    to_owners = jnp.concatenate(
        [
            per_owner(qv_sums, qv_bias.shape),
            per_owner(out_bias_grad.reshape(shares, depth), (depth,)),
            per_owner(up_sums, up_bias.shape),
            per_owner(down_bias_grad.reshape(shares, depth), (depth,)),
            per_owner(two(gain_one, gain_two), norm_gain.shape),
            per_owner(two(shift_one, shift_two), norm_shift.shape),
        ],
        axis=1,
    )
    received = lax.all_to_all(to_owners, ALL, 0, 0, tiled=True)
    mine = jnp.sum(received, axis=0)
    small_owned, at = [], 0
    for shape in small_shapes:
        size = 1
        for length in shape:
            size *= length
        small_owned.append(mine[at : at + size].reshape(shape))
        at += size
    qv_owned, outb_owned, upb_owned, downb_owned, gain_owned, shift_owned = small_owned
    return (
        out,
        in_grad,
        qkv_owned,
        qv_owned,
        out_owned,
        outb_owned,
        up_owned,
        upb_owned,
        down_owned,
        downb_owned,
        gain_owned,
        shift_owned,
    )


def solution(mesh):
    in_specs = (
        P("dp", None),
        P("dp"),
        P(None, "dp", "tensor"),
        P(None, "tensor", "dp"),
        P("tensor", "dp"),
        P("dp"),
        P("dp", "tensor"),
        P("tensor", "dp"),
        P("tensor", "dp"),
        P("dp"),
        P(None, "dp"),
        P(None, "dp"),
        P("dp", None),
    )
    out_specs = (
        P(("dp", "tensor"), None),
        P(("dp", "tensor"), None),
        P(None, "dp", "tensor"),
        P(None, "tensor", "dp"),
        P("tensor", "dp"),
        P("dp"),
        P("dp", "tensor"),
        P("tensor", "dp"),
        P("tensor", "dp"),
        P("dp"),
        P(None, "dp"),
        P(None, "dp"),
    )
    return jax.shard_map(
        per_device, mesh=mesh, in_specs=in_specs, out_specs=out_specs, check_vma=False
    )
```

```python
import functools

import jax
import jax.numpy as jnp
from jax import lax
from jax.experimental import pallas as pl
from jax.experimental.pallas import tpu as pltpu
from jax.sharding import PartitionSpec as P

HD = 64
SEQ = 512
EPSILON = 1e-05
SCALE = HD ** (-0.5)
ALL = ("tensor", "dp")
F32 = jnp.float32
BF16 = jnp.bfloat16


def dot(left, right, left_dim, right_dim):
    return lax.dot_general(
        left, right, (((left_dim,), (right_dim,)), ((), ())), preferred_element_type=F32
    )


def head_part(ref, start):
    return ref[0, :, start : start + HD]


def attend_kernel(width, lengths_ref, proj_ref, context_ref, log_ref):
    length = lengths_ref[pl.program_id(1)]
    valid = lax.broadcasted_iota(jnp.int32, (SEQ, SEQ), 0) < length
    done = []
    for head in range(width // HD):
        at = head * HD
        query = head_part(proj_ref, at) * SCALE
        key = head_part(proj_ref, width + at)
        value = head_part(proj_ref, 2 * width + at)
        scores = jnp.where(valid, dot(key, query, 1, 1), -1000000000.0)
        top = jnp.max(scores, axis=0, keepdims=True)
        expo = jnp.exp(scores - top)
        total = jnp.sum(expo, axis=0, keepdims=True)
        probs = (expo * (1.0 / total)).astype(BF16)
        log_ref[0, 0, head : head + 1, :] = top + jnp.log(total)
        done.append(dot(value, probs, 0, 0))
        if len(done) == 2:
            pair = jnp.concatenate(done, axis=0)
            context_ref[0, :, at - HD : at + HD] = pair.T.astype(BF16)
            done = []


def attend_back_kernel(width, lengths_ref, proj_ref, log_ref, d_context_ref, out_ref):
    length = lengths_ref[pl.program_id(1)]
    valid = lax.broadcasted_iota(jnp.int32, (SEQ, SEQ), 0) < length
    d_query, d_key, d_value = [], [], []
    for head in range(width // HD):
        at = head * HD
        query = head_part(proj_ref, at) * SCALE
        key = head_part(proj_ref, width + at)
        value = head_part(proj_ref, 2 * width + at)
        d_context = head_part(d_context_ref, at)
        scores = jnp.where(valid, dot(key, query, 1, 1), -1000000000.0)
        probs = jnp.exp(scores - log_ref[0, 0, head : head + 1, :])
        d_probs = dot(value, d_context, 1, 1)
        inner = jnp.sum(probs * d_probs, axis=0, keepdims=True)
        d_scores = (probs * (d_probs - inner)).astype(BF16)
        d_query.append(dot(key, d_scores, 0, 0) * SCALE)
        d_key.append(dot(d_scores, query, 1, 0).astype(BF16))
        d_value.append(dot(probs.astype(BF16), d_context, 1, 0).astype(BF16))
        if len(d_query) == 2:
            low, high = at - HD, at + HD
            out_ref[0, :, low:high] = jnp.concatenate(d_query, axis=0).T.astype(BF16)
            out_ref[0, :, width + low : width + high] = jnp.concatenate(d_key, axis=1)
            out_ref[0, :, 2 * width + low : 2 * width + high] = jnp.concatenate(d_value, axis=1)
            d_query, d_key, d_value = [], [], []


def attend(lengths, projected):
    groups, rows, joint = projected.shape
    width = joint // 3
    heads = width // HD
    seqs = rows // SEQ
    return pl.pallas_call(
        functools.partial(attend_kernel, width),
        grid=(groups, seqs),
        in_specs=[
            pl.BlockSpec(memory_space=pltpu.SMEM),
            pl.BlockSpec((1, SEQ, joint), lambda t, s: (t, s, 0)),
        ],
        out_specs=[
            pl.BlockSpec((1, SEQ, width), lambda t, s: (t, s, 0)),
            pl.BlockSpec((1, 1, heads, SEQ), lambda t, s: (t, s, 0, 0)),
        ],
        out_shape=[
            jax.ShapeDtypeStruct((groups, rows, width), BF16),
            jax.ShapeDtypeStruct((groups, seqs, heads, SEQ), F32),
        ],
        compiler_params=pltpu.CompilerParams(vmem_limit_bytes=40 * 1024 * 1024),
        cost_estimate=pl.CostEstimate(
            flops=groups * seqs * heads * 16 * SEQ * SEQ * HD,
            bytes_accessed=groups * rows * joint * 3,
            transcendentals=groups * seqs * heads * SEQ * SEQ,
        ),
    )(lengths, projected)


def attend_back(lengths, projected, log_total, d_context):
    groups, rows, joint = projected.shape
    width = joint // 3
    heads = width // HD
    seqs = rows // SEQ
    return pl.pallas_call(
        functools.partial(attend_back_kernel, width),
        grid=(groups, seqs),
        in_specs=[
            pl.BlockSpec(memory_space=pltpu.SMEM),
            pl.BlockSpec((1, SEQ, joint), lambda t, s: (t, s, 0)),
            pl.BlockSpec((1, 1, heads, SEQ), lambda t, s: (t, s, 0, 0)),
            pl.BlockSpec((1, SEQ, width), lambda t, s: (t, s, 0)),
        ],
        out_specs=pl.BlockSpec((1, SEQ, joint), lambda t, s: (t, s, 0)),
        out_shape=jax.ShapeDtypeStruct((groups, rows, joint), BF16),
        compiler_params=pltpu.CompilerParams(vmem_limit_bytes=40 * 1024 * 1024),
        cost_estimate=pl.CostEstimate(
            flops=groups * seqs * heads * 40 * SEQ * SEQ * HD,
            bytes_accessed=groups * rows * joint * 5,
            transcendentals=groups * seqs * heads * SEQ * SEQ,
        ),
    )(lengths, projected, log_total, d_context)


def row_stats(summed):
    row_mean = jnp.mean(summed, axis=-1, keepdims=True)
    centred = summed - row_mean
    inverse = lax.rsqrt(jnp.mean(centred * centred, axis=-1, keepdims=True) + EPSILON)
    return centred * inverse, inverse


def norm_back(grad_rows, unit_rows, inverse, gain_row):
    scaled = grad_rows * gain_row
    inner = (
        scaled
        - jnp.mean(scaled, axis=-1, keepdims=True)
        - unit_rows * jnp.mean(scaled * unit_rows, axis=-1, keepdims=True)
    )
    return (
        inverse * inner,
        jnp.sum(grad_rows * unit_rows, axis=0),
        jnp.sum(grad_rows, axis=0),
    )


def spread(rows, matrices):
    return jnp.einsum("rd,tdn->trn", rows, matrices, preferred_element_type=F32)


def gather_in(parts, matrices):
    return jnp.einsum("trn,tdn->rd", parts, matrices, preferred_element_type=F32)


def outer(rows, parts):
    return jnp.einsum("rd,trn->tdn", rows, parts, preferred_element_type=F32).astype(BF16)


def per_device(
    tokens_all,
    lengths_all,
    qkv_weight,
    qv_bias,
    out_weight,
    out_bias,
    up_weight,
    up_bias,
    down_weight,
    down_bias,
    norm_gain,
    norm_shift,
    cotangent_all,
):
    groups, shares = lax.axis_size("tensor"), lax.axis_size("dp")
    depth, head_width = qkv_weight.shape[1:]
    width = depth * shares
    hidden_width = up_weight.shape[1]
    rows = tokens_all.shape[0] // groups
    seqs = rows // SEQ
    place = lax.axis_index("tensor")
    tokens = lax.dynamic_slice_in_dim(tokens_all, place * rows, rows, 0)
    cotangent = lax.dynamic_slice_in_dim(cotangent_all, place * rows, rows, 0)
    lengths = lax.dynamic_slice_in_dim(lengths_all, place * seqs, seqs, 0)

    def whole(block):
        full = lax.all_gather(block, ALL, axis=0, tiled=True)
        return full.reshape(groups, width, block.shape[1])

    qkv_block = jnp.transpose(qkv_weight, (1, 0, 2)).reshape(depth, 3 * head_width)
    qkv = whole(qkv_block)
    small_shapes = [
        qv_bias.shape, out_bias.shape, up_bias.shape,
        down_bias.shape, norm_gain.shape, norm_shift.shape,
    ]
    small = jnp.concatenate(
        [a.reshape(-1) for a in (qv_bias, out_bias, up_bias, down_bias, norm_gain, norm_shift)]
    )
    smalls = lax.all_gather(small, ALL, axis=0, tiled=False)
    smalls = smalls.reshape(groups, shares, small.shape[0]).astype(F32)
    cut, at = [], 0
    for shape in small_shapes:
        size = 1
        for length in shape:
            size *= length
        cut.append(smalls[:, :, at : at + size].reshape((groups, shares) + shape))
        at += size
    qv = jnp.transpose(cut[0], (0, 2, 3, 1, 4)).reshape(groups, 2, head_width)
    out_shift = cut[1][0].reshape(width)
    up_shift = jnp.transpose(cut[2], (0, 2, 1, 3)).reshape(groups, hidden_width)
    down_shift = cut[3][0].reshape(width)
    gains = jnp.transpose(cut[4][0], (1, 0, 2)).reshape(2, width)
    shifts = jnp.transpose(cut[5][0], (1, 0, 2)).reshape(2, width)

    rest = whole(jnp.concatenate([out_weight.T, up_weight, down_weight.T], axis=1))
    out_full = rest[:, :, :head_width]
    up_full = rest[:, :, head_width : head_width + hidden_width]
    down_full = rest[:, :, head_width + hidden_width :]

    qkv_bias = jnp.concatenate([qv[:, 0], jnp.zeros_like(qv[:, 0]), qv[:, 1]], axis=1)
    projected = (spread(tokens, qkv) + qkv_bias[:, None, :]).astype(BF16)
    context, log_total = attend(lengths, projected)

    attended = gather_in(context, out_full)
    unit_one, inverse_one = row_stats(tokens.astype(F32) + attended + out_shift)
    normed_one = unit_one * gains[0] + shifts[0]
    normed_one_b = normed_one.astype(BF16)
    pre_act = spread(normed_one_b, up_full) + up_shift[:, None, :]
    hidden = jax.nn.gelu(pre_act, approximate=False).astype(BF16)
    ffn_out = gather_in(hidden, down_full)
    unit_two, inverse_two = row_stats(normed_one + ffn_out + down_shift)
    out = (unit_two * gains[1] + shifts[1]).astype(BF16)

    positions = lax.iota(jnp.int32, SEQ)
    row_valid = (positions[None, :] < lengths[:, None]).astype(F32).reshape(rows, 1)
    d_out = cotangent.astype(F32) * row_valid
    d_sum_two, gain_two, shift_two = norm_back(d_out, unit_two, inverse_two, gains[1])
    d_ffn = d_sum_two.astype(BF16)
    down_bias_grad = jnp.sum(d_sum_two, axis=0)

    def owned(grad):
        blocks = grad.reshape(groups, shares, depth, grad.shape[2])
        flat = jnp.transpose(blocks, (1, 0, 2, 3)).reshape(groups * width, grad.shape[2])
        return lax.psum_scatter(
            flat, ("dp", "tensor"), scatter_dimension=0, tiled=True
        ).astype(F32)

    down_owned = owned(outer(d_ffn, hidden)).T
    d_hidden = spread(d_ffn, down_full)
    _, gelu_pull = jax.vjp(lambda inner: jax.nn.gelu(inner, approximate=False), pre_act)
    d_pre = gelu_pull(d_hidden)[0].astype(BF16)
    up_bias_grad = jnp.sum(d_pre.astype(F32), axis=1)
    up_grad = outer(normed_one_b, d_pre)
    d_normed_one = d_sum_two + gather_in(d_pre, up_full)
    d_sum_one, gain_one, shift_one = norm_back(d_normed_one, unit_one, inverse_one, gains[0])
    d_attn = d_sum_one.astype(BF16)
    out_bias_grad = jnp.sum(d_sum_one, axis=0)
    out_grad = outer(d_attn, context)
    d_context = spread(d_attn, out_full).astype(BF16)
    d_joined = attend_back(lengths, projected, log_total, d_context)
    qkv_grad = outer(tokens, d_joined)
    rest_owned = owned(jnp.concatenate([up_grad, out_grad, qkv_grad], axis=2))
    up_owned = rest_owned[:, :hidden_width]
    out_owned = rest_owned[:, hidden_width : hidden_width + head_width].T
    qkv_owned = jnp.transpose(
        rest_owned[:, hidden_width + head_width :].reshape(depth, 3, head_width), (1, 0, 2)
    )
    in_grad = d_sum_one + gather_in(d_joined, qkv)

    joined_sums = jnp.sum(d_joined.astype(F32), axis=1).reshape(groups, 3, head_width)
    qv_sums = jnp.stack([joined_sums[:, 0], joined_sums[:, 2]], axis=1)

    def per_owner(array, shape):
        return jnp.broadcast_to(array, (groups, shares) + shape).reshape(groups * shares, -1)

    heads, piece = qv_bias.shape[1:]
    unit_rows, unit_piece = up_bias.shape
    qv_sums = jnp.transpose(qv_sums.reshape(groups, 2, heads, shares, piece), (0, 3, 1, 2, 4))
    up_sums = jnp.transpose(up_bias_grad.reshape(groups, unit_rows, shares, unit_piece), (0, 2, 1, 3))
    two = lambda one, other: jnp.transpose(
        jnp.stack([one, other]).reshape(2, shares, depth), (1, 0, 2)
    )
    to_owners = jnp.concatenate(
        [
            per_owner(qv_sums, qv_bias.shape),
            per_owner(out_bias_grad.reshape(shares, depth), (depth,)),
            per_owner(up_sums, up_bias.shape),
            per_owner(down_bias_grad.reshape(shares, depth), (depth,)),
            per_owner(two(gain_one, gain_two), norm_gain.shape),
            per_owner(two(shift_one, shift_two), norm_shift.shape),
        ],
        axis=1,
    )
    received = lax.all_to_all(to_owners, ALL, 0, 0, tiled=True)
    mine = jnp.sum(received, axis=0)
    small_owned, at = [], 0
    for shape in small_shapes:
        size = 1
        for length in shape:
            size *= length
        small_owned.append(mine[at : at + size].reshape(shape))
        at += size
    qv_owned, outb_owned, upb_owned, downb_owned, gain_owned, shift_owned = small_owned
    return (
        out,
        in_grad,
        qkv_owned,
        qv_owned,
        out_owned,
        outb_owned,
        up_owned,
        upb_owned,
        down_owned,
        downb_owned,
        gain_owned,
        shift_owned,
    )


def solution(mesh):
    in_specs = (
        P("dp", None),
        P("dp"),
        P(None, "dp", "tensor"),
        P(None, "tensor", "dp"),
        P("tensor", "dp"),
        P("dp"),
        P("dp", "tensor"),
        P("tensor", "dp"),
        P("tensor", "dp"),
        P("dp"),
        P(None, "dp"),
        P(None, "dp"),
        P("dp", None),
    )
    out_specs = (
        P(("dp", "tensor"), None),
        P(("dp", "tensor"), None),
        P(None, "dp", "tensor"),
        P(None, "tensor", "dp"),
        P("tensor", "dp"),
        P("dp"),
        P("dp", "tensor"),
        P("tensor", "dp"),
        P("tensor", "dp"),
        P("dp"),
        P(None, "dp"),
        P(None, "dp"),
    )
    return jax.shard_map(
        per_device, mesh=mesh, in_specs=in_specs, out_specs=out_specs, check_vma=False
    )
```
